32 devices in a mesh: grp: 2 (over x), dp: 16 (over z, y, core).
Axes of the slice: x: 2, y: 2, z: 4, core: 2. Of those that a mesh axis runs over, the one named last changes fastest.
Arguments:
- teacher_in: bfloat16 [8192, 1664], P('dp'), may hold values from -6 to 6
- teacher_gain: float32 [1664], replicated, may hold values from 0.5 to 1.5
- teacher_up: bfloat16 [1664, 4096], P('dp', 'grp'), may hold values from -0.15625 to 0.15625
- teacher_down: bfloat16 [1664, 4096], P('dp', 'grp'), may hold values from -0.09375 to 0.09375
- student_in: bfloat16 [8192, 768], P('dp'), may hold values from -6 to 6
- student_gain: float32 [768], replicated, may hold values from 0.5 to 1.5
- student_up: bfloat16 [768, 1536], P(None, ('grp', 'dp')), may hold values from -0.21875 to 0.21875
- student_down: bfloat16 [1536, 768], P(('grp', 'dp')), may hold values from -0.15625 to 0.15625
- student_head: bfloat16 [768, 1664], P(None, ('grp', 'dp')), may hold values from -0.21875 to 0.21875
- student_proj: bfloat16 [768, 512], P(None, ('grp', 'dp')), may hold values from -1 to 1
- word_table: bfloat16 [49408, 512], P(('grp', 'dp')), may hold values from -6 to 6
- caption_ids: int32 [32, 77], replicated, may hold values from 0 to 49407
- positive: int32 [32], replicated, may hold values from 0 to 31, each once
Outputs:
- loss: float32 [], replicated
- grad_up: float32 [768, 1536], P(None, ('grp', 'dp'))
- grad_down: float32 [1536, 768], P(('grp', 'dp'))
- grad_head: float32 [768, 1664], P(None, ('grp', 'dp'))
- grad_proj: float32 [768, 512], P(None, ('grp', 'dp'))
The draws below stay inside these ranges and needn't reach their ends.
Inputs may be any that keep to these rules, and one draw needn't show every extreme that they name: Each caption is the positive of exactly one image.
All inputs are finite; a program needn't handle non-finite values.
Results may differ from the reference program's by a relative error of at most 0.0065.
Values may be sent and summed in bfloat16 or wider, within the bound.
No kernel may reach another device: no remote copies, remote signals or barrier semaphores. Data moves between devices by JAX's collectives and lax.ppermute only.
A program may use at most 128 MiB of HBM per device.

```python
import math
import jax
import jax.numpy as jnp
import numpy as np
from jax import lax

DT = 1664
HT = 4096
DS = 768
HS = 1536
DE = 512
VOCAB = 49408
CAP_LEN = 77
PATCHES = 256
IMAGES = 32
CAPTIONS = 32
N_GRP = 2
N_DP = 16


def draw_student_in(key, part):
    noise_key = jax.random.fold_in(key, 1103)
    values = jax.random.normal(noise_key, (IMAGES * PATCHES, DS), jnp.float32)
    return jnp.clip(values, -6.0, 6.0).astype(jnp.bfloat16)


def draw_student_proj(key, part):
    noise_key = jax.random.fold_in(key, 2207)
    values = jax.random.normal(noise_key, (DS, DE), jnp.float32) / jnp.sqrt(jnp.float32(DS))
    return jnp.clip(values, -1.0, 1.0).astype(jnp.bfloat16)


def draw_word_table(key, part):
    noise_key = jax.random.fold_in(key, 3301)
    values = jax.random.normal(noise_key, (VOCAB, DE), jnp.float32)
    return jnp.clip(values, -6.0, 6.0).astype(jnp.bfloat16)


def place_ends(values, key, low, top_value):
    longest = values.shape.index(max(values.shape))
    spots = []
    for shift in (0, 1):
        where = [jax.random.randint(jax.random.fold_in(key, axis), (), 0, length) for axis, length in enumerate(values.shape)]
        where[longest] = (where[longest] + shift) % values.shape[longest]
        spots.append(tuple(where))
    return values.at[spots[0]].set(low).at[spots[1]].set(top_value)


def levels(rng, shape, cuts, low, high):
    level, own = 1.0, jax.random.fold_in(rng, 6)
    for axis_at, blocks in cuts:
        heights = jnp.exp(jax.random.uniform(jax.random.fold_in(own, axis_at), (blocks,), jnp.float32, low / len(cuts), high / len(cuts)))
        level = level * jnp.repeat(heights, shape[axis_at] // blocks).reshape([-1 if axis == axis_at else 1 for axis in range(len(shape))])
    return level


def rank_bounds(number_of, slope):
    portions = [(1 << 20) // math.isqrt(rank ** slope) + 1 for rank in range(1, number_of + 1)]
    scale = 1 + sum(portions) // (1 << 30)
    return np.cumsum(np.array([max(1, weight // scale) for weight in portions]))


def ranked(key, dims, number_of, skew):
    table = rank_bounds(number_of, skew)
    pick = jax.random.randint(jax.random.fold_in(key, 1), dims, 0, int(table[number_of - 1]))
    rank = jnp.searchsorted(jnp.asarray(table, jnp.int32), pick, side="right")
    return jax.random.permutation(jax.random.fold_in(key, 2), number_of)[rank].astype(jnp.int32)


def gaussian(key, shape, scale, limit, cuts=(), held_as=jnp.bfloat16):
    loudness = levels(key, shape, cuts, -0.22, 0.18) if cuts else 1.0
    values = jax.random.normal(key, shape, jnp.float32) * scale * loudness
    return jnp.minimum(jnp.maximum(values, -limit), limit).astype(held_as)


def setup_inputs(seed: int = 0) -> dict:
    key_list = jax.random.split(jax.random.key(seed), 14)
    return {
        "teacher_in": gaussian(key_list[0], (IMAGES * PATCHES, DT), 1.0, 6.0, ((0, 16),)),
        "teacher_gain": jnp.clip(1.0 + 0.1 * jax.random.normal(key_list[1], (DT,), jnp.float32), 0.5, 1.5),
        "teacher_up": gaussian(key_list[2], (DT, HT), DT ** -0.5, 0.15625, ((0, 16), (1, 2))),
        "teacher_down": gaussian(key_list[3], (DT, HT), HT ** -0.5, 0.09375, ((0, 16), (1, 2))),
        "student_in": draw_student_in(jax.random.fold_in(key_list[13], 71), 0),
        "student_gain": jnp.clip(1.0 + 0.1 * jax.random.normal(key_list[5], (DS,), jnp.float32), 0.5, 1.5),
        "student_up": gaussian(key_list[6], (DS, HS), DS ** -0.5, 0.21875, ((1, 32),)),
        "student_down": gaussian(key_list[7], (HS, DS), HS ** -0.5, 0.15625, ((0, 32),)),
        "student_head": gaussian(key_list[8], (DS, DT), DS ** -0.5, 0.21875, ((1, 32),)),
        "student_proj": draw_student_proj(jax.random.fold_in(key_list[13], 71), 0),
        "word_table": draw_word_table(jax.random.fold_in(key_list[13], 71), 0),
        "caption_ids": place_ends(ranked(key_list[11], (CAPTIONS, CAP_LEN), VOCAB, 2), jax.random.fold_in(key_list[11], 3), 0, VOCAB - 1).astype(jnp.int32),
        "positive": jax.random.permutation(key_list[12], IMAGES).astype(jnp.int32),
    }


def normalize_rows(values, gain):
    center = values - lax.optimization_barrier(jnp.mean(values, -1, keepdims=True))
    spread = lax.optimization_barrier(jnp.mean(center * center, -1, keepdims=True))
    return center * lax.rsqrt(spread + 1e-05) * gain

def gelu_tanh(values):
    return jax.nn.gelu(values, approximate=True)

def unit_rows(values):
    return values / jnp.sqrt(lax.optimization_barrier(jnp.sum(values * values, -1, keepdims=True)) + 1e-06)

def reference(teacher_in, teacher_gain, teacher_up, teacher_down, student_in, student_gain, student_up, student_down, student_head, student_proj, word_table, caption_ids, positive):
    half_units = HT // N_GRP
    contract = (((1,), (1,)), ((), ()))

    def teacher_block(rows):
        normed = normalize_rows(rows.astype(jnp.float32), teacher_gain).astype(jnp.bfloat16)
        hidden = jnp.dot(normed, teacher_up, preferred_element_type=jnp.float32)
        active = gelu_tanh(hidden).astype(jnp.bfloat16)
        branch = jnp.zeros((rows.shape[0], DT), jnp.float32)
        for group in range(N_GRP):
            part = lax.dot_general(active[:, group * half_units:(group + 1) * half_units], teacher_down[:, group * half_units:(group + 1) * half_units], contract, preferred_element_type=jnp.float32)
            rounded = lax.optimization_barrier(part.astype(jnp.bfloat16))
            branch = branch + rounded.astype(jnp.float32)
        return rows.astype(jnp.float32) + branch
    target = lax.map(teacher_block, teacher_in.reshape(N_DP, -1, DT)).reshape(-1, DT)
    student_rows = student_in.astype(jnp.float32)
    student_normed = normalize_rows(student_rows, student_gain).astype(jnp.bfloat16)
    gate_out = jnp.dot(student_normed, student_up, preferred_element_type=jnp.float32)
    student_act = gelu_tanh(gate_out).astype(jnp.bfloat16)
    student_out = student_rows + jnp.dot(student_act, student_down, preferred_element_type=jnp.float32)
    student_rounded = student_out.astype(jnp.bfloat16)
    diff = jnp.dot(student_rounded, student_head, preferred_element_type=jnp.float32) - target
    feature_total = jnp.sum(diff * diff) / DT
    pooled = (lax.optimization_barrier(jnp.sum(student_out.reshape(IMAGES, PATCHES, DS), 1)) / PATCHES).astype(jnp.bfloat16)
    projected = jnp.dot(pooled, student_proj, preferred_element_type=jnp.float32)
    proj_norm = jnp.sqrt(lax.optimization_barrier(jnp.sum(projected * projected, -1, keepdims=True)) + 1e-06)
    image_emb = projected / proj_norm
    caption_sum = lax.optimization_barrier(jnp.sum(word_table[caption_ids].astype(jnp.float32), 1)) / CAP_LEN
    caption_emb = unit_rows(caption_sum)
    scores = 100.0 * jnp.dot(image_emb, caption_emb.T, precision=lax.Precision.HIGHEST)
    match = (positive[:, None] == jnp.arange(CAPTIONS, dtype=jnp.int32)[None, :]).astype(jnp.float32)
    contrast_total = jnp.sum(jax.nn.logsumexp(scores, 1)) + jnp.sum(jax.nn.logsumexp(scores, 0)) - 2.0 * jnp.sum(match * scores)
    loss = (feature_total + contrast_total) / (IMAGES * PATCHES)
    grad_scores = jax.nn.softmax(scores, 1) + jax.nn.softmax(scores, 0) - 2.0 * match
    grad_image = 100.0 * jnp.dot(grad_scores, caption_emb, precision=lax.Precision.HIGHEST)
    grad_projected = ((grad_image - image_emb * lax.optimization_barrier(jnp.sum(image_emb * grad_image, -1, keepdims=True))) / proj_norm).astype(jnp.bfloat16)
    grad_proj = jnp.dot(pooled.T, grad_projected, preferred_element_type=jnp.float32)
    grad_pooled = jnp.dot(grad_projected, student_proj.T, preferred_element_type=jnp.float32)
    grad_pred = (2.0 * diff / DT).astype(jnp.bfloat16)
    grad_head = jnp.dot(student_rounded.T, grad_pred, preferred_element_type=jnp.float32)
    grad_out = jnp.dot(grad_pred, student_head.T, preferred_element_type=jnp.float32)
    grad_out = (grad_out.reshape(IMAGES, PATCHES, DS) + (grad_pooled / PATCHES)[:, None, :]).reshape(-1, DS).astype(jnp.bfloat16)
    grad_down = jnp.dot(student_act.T, grad_out, preferred_element_type=jnp.float32)
    grad_act = jnp.dot(grad_out, student_down.T, preferred_element_type=jnp.float32)
    grad_gate = jax.vjp(gelu_tanh, gate_out)[1](grad_act)[0].astype(jnp.bfloat16)
    grad_up = jnp.dot(student_normed.T, grad_gate, preferred_element_type=jnp.float32)
    return (loss, grad_up, grad_down, grad_head, grad_proj)
```

```python
import jax
import jax.numpy as jnp
from jax import lax
from jax.sharding import PartitionSpec as P

CAP_LEN = 77
PATCHES = 256
BOTH = ("grp", "dp")
BF16 = jnp.bfloat16
F32 = jnp.float32


def normalize_rows(values, gain):
    center = values - jnp.mean(values, -1, keepdims=True)
    spread = jnp.mean(center * center, -1, keepdims=True)
    return center * lax.rsqrt(spread + 1e-05) * gain


def gelu_tanh(values):
    return jax.nn.gelu(values, approximate=True)


def unit_rows(values):
    return values / jnp.sqrt(jnp.sum(values * values, -1, keepdims=True) + 1e-06)


def dot(a, b, ca, cb, out=F32):
    return lax.dot_general(a, b, (((ca,), (cb,)), ((), ())), preferred_element_type=F32).astype(out)


def exact(a, b, ca, cb):
    return lax.dot_general(
        a, b, (((ca,), (cb,)), ((), ())), precision=lax.Precision.HIGHEST, preferred_element_type=F32
    )


def pick(values, index, size, axis=0):
    return lax.dynamic_slice_in_dim(values, index * size, size, axis)


def local(
    teacher_in,
    teacher_gain,
    teacher_up,
    teacher_down,
    student_in,
    student_gain,
    student_up,
    student_down,
    student_head,
    student_proj,
    word_table,
    caption_ids,
    positive,
):
    grp = lax.axis_index("grp")
    dp = lax.axis_index("dp")
    n_grp = lax.axis_size("grp")
    n_dp = lax.axis_size("dp")
    devices = n_grp * n_dp
    n_z = n_dp // 4
    core = dp % 2
    chip = dp // 2
    y = chip % 2
    z = chip // 2
    me = grp * n_dp + dp
    MASK_C, MASK_Y, MASK_X = 1, 2, n_dp

    def swap(values, mask):
        return lax.ppermute(values, BOTH, [(i, i ^ mask) for i in range(devices)])

    rows_w, hidden_w = teacher_up.shape
    half_w = hidden_w // 2
    weights = jnp.concatenate([teacher_up, teacher_down], 0)
    kept = pick(weights, core, half_w, 1)
    came = swap(pick(weights, 1 - core, half_w, 1), MASK_C)
    first = jnp.where(core == 0, kept, came)
    second = jnp.where(core == 0, came, kept)
    up_pair = jnp.concatenate([first[:rows_w], second[:rows_w]], 0)
    down_pair = jnp.concatenate([first[rows_w:], second[rows_w:]], 0)

    n_up = student_up.shape[1]
    n_down = student_down.shape[0]
    n_proj = student_proj.shape[1]
    n_head = student_head.shape[1]
    width = student_in.shape[1]
    n_rows = n_up + n_down + n_proj + n_head
    block = jnp.concatenate(
        [
            student_up.T,
            student_down,
            student_proj.T,
            student_head.T,
            jnp.zeros((-n_rows % 8, width), BF16),
        ],
        0,
    )

    def spread_zy(own):
        along = [own] + [swap(own, 4 * k) for k in range(1, n_z)]
        return [w for v in along for w in (v, swap(v, MASK_Y))]

    blocks = spread_zy(block)
    blocks = jnp.stack(blocks + [swap(v, MASK_X) for v in blocks])
    blocks = jnp.stack([blocks, swap(blocks, MASK_C)])
    blocks = blocks.reshape(devices, -1, width)
    up_t = blocks[:, :n_up].reshape(devices * n_up, width)
    down_w = blocks[:, n_up : n_up + n_down].reshape(devices * n_down, width)
    proj_rel = blocks[:, n_up + n_down : n_up + n_down + n_proj].reshape(devices * n_proj, width)
    head_rel = blocks[:, n_up + n_down + n_proj : n_rows].reshape(devices * n_head, width)

    def owner(position):
        mask = (position // n_dp) * MASK_C + ((position // (n_dp // 2)) % 2) * MASK_X
        return (mask + (position % (n_dp // 2)) * 2) ^ me

    def where_from(length, size):
        place = jnp.arange(length, dtype=jnp.int32)
        return owner(place // size) * size + place % size

    up_all = jnp.concatenate(spread_zy(up_pair), 0)
    downs = spread_zy(down_pair)
    n_chips = len(downs)
    down_groups = [
        jnp.concatenate(downs[: n_chips // 2], 0),
        jnp.concatenate(downs[n_chips // 2 :], 0),
    ]
    pair = 2 * rows_w

    t_width = teacher_in.shape[1]
    place = jnp.arange(t_width, dtype=jnp.int32)
    canon = ((place // pair) ^ chip) * pair + place % pair
    rows_t = teacher_in.shape[0]
    own_rows = rows_t // n_grp
    t_own = pick(teacher_in, grp, own_rows)
    t_normed = normalize_rows(teacher_in.astype(F32), teacher_gain).astype(BF16)
    order = (place[:, None] == canon[None, :]).astype(BF16)
    t_normed = dot(t_normed, order, 1, 0, BF16)
    half_t = t_width // 2
    t_own_g = [dot(t_own, order[:, g * half_t : (g + 1) * half_t], 1, 0) for g in range(2)]
    t_rows = jnp.concatenate([t_normed, swap(t_normed, MASK_C)], 0)

    caption_count = caption_ids.shape[0]
    vocab_dev = word_table.shape[0]
    codes = me * vocab_dev + jnp.arange(vocab_dev, dtype=jnp.int32)
    counts = jnp.sum(
        caption_ids[:, :, None] == codes[None, None, :], 1, dtype=F32
    ).astype(BF16)
    words = dot(counts, word_table, 1, 0)
    embed = words.shape[1]
    words = lax.all_to_all(words.reshape(devices, -1, embed), BOTH, 0, 0)
    caption_own = jnp.sum(words, 0) / CAP_LEN

    s_rows = pick(student_in, grp, own_rows).astype(F32)
    s_normed = normalize_rows(s_rows, student_gain).astype(BF16)
    gate = dot(s_normed, up_t, 1, 1)
    s_act = gelu_tanh(gate).astype(BF16)
    s_out = s_rows + dot(s_act, down_w, 1, 0)
    s_round = s_out.astype(BF16)
    n_img = own_rows // PATCHES
    pooled = (jnp.sum(s_out.reshape(n_img, PATCHES, width), 1) / PATCHES).astype(BF16)

    sent = jnp.concatenate([pooled.astype(F32).reshape(-1), caption_own.reshape(-1)])
    got = lax.all_to_all(jnp.broadcast_to(sent[None], (devices,) + sent.shape), BOTH, 0, 0)
    pooled_all = got[:, : n_img * width].reshape(-1, width).astype(BF16)
    caption = unit_rows(got[:, n_img * width :].reshape(caption_count, embed))
    place_e = jnp.arange(embed, dtype=jnp.int32)
    order_e = (place_e[:, None] == where_from(embed, n_proj)[None, :]).astype(BF16)
    proj_t = dot(order_e, proj_rel, 1, 0, BF16)
    projected = dot(pooled_all, proj_t, 1, 1)
    proj_norm = jnp.sqrt(jnp.sum(projected * projected, -1, keepdims=True) + 1e-06)
    image = projected / proj_norm
    wanted = jnp.transpose(positive.reshape(n_dp, n_grp, n_img), (1, 0, 2)).reshape(-1)
    match = (wanted[:, None] == jnp.arange(caption_count, dtype=jnp.int32)[None, :]).astype(F32)
    scores = 100.0 * exact(image, caption, 1, 1)
    contrast = (
        jnp.sum(jax.nn.logsumexp(scores, 1))
        + jnp.sum(jax.nn.logsumexp(scores, 0))
        - 2.0 * jnp.sum(match * scores)
    )
    grad_scores = jax.nn.softmax(scores, 1) + jax.nn.softmax(scores, 0) - 2.0 * match
    grad_image = 100.0 * exact(grad_scores, caption, 1, 0)
    grad_projected = (
        (grad_image - image * jnp.sum(image * grad_image, -1, keepdims=True)) / proj_norm
    ).astype(BF16)
    grad_proj = dot(pick(grad_projected, me, n_proj, 1), pooled_all, 0, 0).T
    grad_pooled = dot(pick(grad_projected, me, n_img), proj_t, 1, 0)

    from_h = where_from(t_width, n_head)
    order_h = (canon[:, None] == from_h[None, :]).astype(BF16)
    head_t = dot(order_h, head_rel, 1, 0, BF16)
    head_g = [head_t[g * half_t : (g + 1) * half_t] for g in range(2)]

    t_act = gelu_tanh(dot(t_rows, up_all, 1, 0)).astype(BF16)
    diffs = []
    for g in range(2):
        far = swap(dot(t_act[rows_t:], down_groups[g], 1, 1, BF16), MASK_C)
        part = (dot(t_act[:rows_t], down_groups[g], 1, 1) + far.astype(F32)).astype(BF16)
        other = swap(pick(part, 1 - grp, own_rows), MASK_X)
        target = t_own_g[g] + (pick(part, grp, own_rows).astype(F32) + other.astype(F32))
        diffs.append(dot(s_round, head_g[g], 1, 1) - target)
    feature = (jnp.sum(diffs[0] * diffs[0]) + jnp.sum(diffs[1] * diffs[1])) / t_width

    preds = [(2.0 * d / t_width).astype(BF16) for d in diffs]
    half_s = width // 2
    s_mine = pick(s_round, core, half_s, 1)
    s_their = pick(s_round, 1 - core, half_s, 1)
    head_parts = []
    for g in range(2):
        far = swap(dot(preds[g], s_their, 0, 0, BF16), MASK_C)
        head_parts.append(dot(preds[g], s_mine, 0, 0) + far.astype(F32))
    top = chip // n_z
    low = chip % n_z
    mine = (grp ^ top) == 0
    head_keep = jnp.where(mine, head_parts[0], head_parts[1])
    head_send = jnp.where(mine, head_parts[1], head_parts[0]).astype(BF16)
    head_sum = head_keep + swap(head_send, MASK_X).astype(F32)
    head_sum = head_sum.reshape(n_z, -1, half_s)
    head_bits = head_sum.astype(BF16)
    total = pick(head_sum, z ^ low, 1)[0]
    for k in range(1, n_z):
        total = total + swap(pick(head_bits, z ^ k ^ low, 1)[0], 4 * k).astype(F32)
    total = total.reshape(2, -1, half_s)
    total = pick(total, y, 1)[0] + swap(pick(total, 1 - y, 1)[0].astype(BF16), MASK_Y).astype(F32)
    total = total.reshape(2, n_head, half_s)
    kept = pick(total, core, 1)[0]
    came = swap(pick(total, 1 - core, 1)[0], MASK_C)
    grad_head = jnp.where(
        core == 0, jnp.concatenate([kept, came], 1), jnp.concatenate([came, kept], 1)
    ).T

    grad_out = dot(preds[0], head_g[0], 1, 0) + dot(preds[1], head_g[1], 1, 0)
    grad_out = (
        (grad_out.reshape(n_img, PATCHES, width) + (grad_pooled / PATCHES)[:, None, :])
        .reshape(-1, width)
        .astype(BF16)
    )

    def scatter(left, right, size, first_x):
        half = left.shape[1] // 2
        far = swap(dot(left[:, half:], right, 0, 0, BF16), MASK_C)
        sums = dot(left[:, :half], right, 0, 0) + far.astype(F32)
        sums = sums.reshape(2, n_z, 2, size, width)
        if first_x:
            sums = sums[0] + swap(sums[1].astype(BF16), MASK_X).astype(F32)
            sums = sums[:, 0] + swap(sums[:, 1].astype(BF16), MASK_Y).astype(F32)
        else:
            sums = sums[:, :, 0] + swap(sums[:, :, 1].astype(BF16), MASK_Y).astype(F32)
            sums = sums[0] + swap(sums[1].astype(BF16), MASK_X).astype(F32)
        out = sums[0]
        for k in range(1, n_z):
            out = out + swap(sums[k].astype(BF16), 4 * k).astype(F32)
        return out

    grad_down = scatter(s_act, grad_out, n_down, False)
    grad_act = dot(grad_out, down_w, 1, 1)
    grad_gate = jax.vjp(gelu_tanh, gate)[1](grad_act)[0].astype(BF16)
    grad_up = scatter(grad_gate, s_normed, n_up, True).T

    mask = 1
    feature = jnp.broadcast_to(feature, (8, 128))
    while mask < devices:
        feature = feature + swap(feature, mask)
        mask *= 2
    loss = (feature[0, 0] + contrast) / (positive.shape[0] * PATCHES)
    return (loss, grad_up, grad_down, grad_head, grad_proj)


def solution(mesh):
    placed = (
        P("dp", None),
        P(),
        P("dp", "grp"),
        P("dp", "grp"),
        P("dp", None),
        P(),
        P(None, BOTH),
        P(BOTH, None),
        P(None, BOTH),
        P(None, BOTH),
        P(BOTH, None),
        P(),
        P(),
    )
    return jax.shard_map(
        local,
        mesh=mesh,
        in_specs=placed,
        out_specs=(
            P(),
            P(None, BOTH),
            P(BOTH, None),
            P(None, BOTH),
            P(None, BOTH),
        ),
        check_vma=False,
    )
```

```python
import jax
import jax.numpy as jnp
from jax import lax
from jax.sharding import PartitionSpec as P

CAP_LEN = 77
WINDOW = 7
PATCHES = 256
BOTH = ("grp", "dp")
BF16 = jnp.bfloat16
F32 = jnp.float32


def normalize_rows(values, gain):
    center = values - jnp.mean(values, -1, keepdims=True)
    spread = jnp.mean(center * center, -1, keepdims=True)
    return center * lax.rsqrt(spread + 1e-05) * gain


def gelu_tanh(values):
    return jax.nn.gelu(values, approximate=True)


def unit_rows(values):
    return values / jnp.sqrt(jnp.sum(values * values, -1, keepdims=True) + 1e-06)


def dot(a, b, ca, cb, out=F32):
    return lax.dot_general(a, b, (((ca,), (cb,)), ((), ())), preferred_element_type=F32).astype(out)


def exact(a, b, ca, cb):
    return lax.dot_general(
        a, b, (((ca,), (cb,)), ((), ())), precision=lax.Precision.HIGHEST, preferred_element_type=F32
    )


def pick(values, index, size, axis=0):
    return lax.dynamic_slice_in_dim(values, index * size, size, axis)


def after(values, *first):
    return lax.optimization_barrier((values,) + first)[0]


def local(
    teacher_in,
    teacher_gain,
    teacher_up,
    teacher_down,
    student_in,
    student_gain,
    student_up,
    student_down,
    student_head,
    student_proj,
    word_table,
    caption_ids,
    positive,
):
    grp = lax.axis_index("grp")
    dp = lax.axis_index("dp")
    n_grp = lax.axis_size("grp")
    n_dp = lax.axis_size("dp")
    devices = n_grp * n_dp
    n_z = n_dp // 4
    n_chips = n_dp // 2
    core = dp & 1
    chip = dp >> 1
    y = chip & 1
    z = chip >> 1
    me = grp * n_dp + dp
    MASK_C, MASK_Y, MASK_X = 1, 2, n_dp
    top = chip // n_z
    low = chip & (n_z - 1)

    def swap(values, mask):
        return lax.ppermute(values, BOTH, [(i, i ^ mask) for i in range(devices)])

    line = []

    def queued(values, mask, *first):
        first = first + tuple(line[: len(line) - WINDOW + 1][-6:] if len(line) >= WINDOW else ())
        if first:
            values = after(values, *first)
        line.append(swap(values, mask))
        return line[-1]

    def put(buffer, values, index):
        return lax.dynamic_update_slice(
            buffer, values[None], (index,) + (0,) * (buffer.ndim - 1)
        )

    width = student_in.shape[1]
    n_head = student_head.shape[1]
    tile = n_head + 8 - n_head % 8
    rows_w, hidden_w = teacher_up.shape
    half_w = hidden_w // 2
    at = jnp.arange(2 * tile, dtype=jnp.int32)
    at = jnp.where(at % tile < n_head, (at // tile) * n_head + at % tile, -1)
    widen = (at[:, None] == jnp.arange(rows_w, dtype=jnp.int32)[None, :]).astype(BF16)
    send_up = pick(teacher_up, 1 - core, half_w, 1)
    down_rows = lax.optimization_barrier(dot(widen, teacher_down, 1, 0, BF16))
    send_down = pick(down_rows, 1 - core, half_w, 1)
    far_up, far_down, far_in = swap(send_up, MASK_C), swap(send_down, MASK_C), swap(teacher_in, MASK_C)
    own_up = pick(teacher_up, core, half_w, 1)
    own_down = pick(down_rows, core, half_w, 1)

    def in_order(mine, other):
        return jnp.stack([jnp.where(core == 0, mine, other), jnp.where(core == 0, other, mine)])

    up_pair = in_order(own_up, far_up).reshape(2 * rows_w, half_w)
    down_pair = in_order(own_down, far_down).reshape(4 * tile, half_w)

    n_up = student_up.shape[1]
    n_down = student_down.shape[0]
    n_proj = student_proj.shape[1]
    head_rows = dot(widen[:tile, :n_head], student_head, 1, 1, BF16)
    block = jnp.concatenate(
        [
            after(student_up, send_up, send_down).T,
            student_down,
            student_proj.T,
            head_rows,
        ],
        0,
    )

    half = devices // 2
    place_own = (me ^ (4 * chip)) >> 2
    if n_z == 4:
        rounds = [
            [("z", "s", 3), ("z", "s", 1), ("y", "s", 0), ("y", "u", 0)],
            [("z", "u", 3), ("z", "s", 2), ("y", "s", 3), ("y", "s", 1), ("x", "s", (0,))],
            [("z", "u", 1), ("z", "u", 2), ("y", "s", 2), ("y", "u", 3), ("x", "s", (1, 3))],
            [("z", "d", 3), ("z", "d", 1), ("y", "u", 1), ("y", "u", 2), ("x", "s", (2,))],
            [("c", "s", 0), ("z", "d", 2), ("y", "d", 0), ("y", "d", 1), ("y", "d", 3)],
            [("y", "d", 2)],
        ]
    else:
        some = [("z", p, j) for p in "sud" for j in range(1, n_z)]
        some += [("y", p, j) for p in "sud" for j in range(n_z)]
        some += [("x", "s", (j,)) for j in range(n_z)] + [("c", "s", 0)]
        some += [some.pop(some.index(("y", "d", n_z - 1)))]
        rounds = [some[i : i + 1] for i in range(len(some))]
    held = {("z", "s", 0): block, ("z", "u", 0): up_pair, ("z", "d", 0): down_pair}
    stack, placed = [None], []

    def values_of(axis, name, j):
        if axis == "z" and n_z == 4 and j == 2:
            return held["z", name, 3], 4
        if axis == "z":
            return held["z", name, 0], 4 * j
        if axis == "y":
            return held["z", name, j], MASK_Y
        if axis == "x":
            both = []
            for k in j:
                mine, theirs = held["z", name, k], held["y", name, k]
                both += [jnp.where(y == 0, mine, theirs), jnp.where(y == 0, theirs, mine)]
            held["both", name, j] = jnp.stack(both)
            return held["both", name, j], MASK_X
        return stack[0], MASK_C

    def run(batch, *first):
        todo = [values_of(*item) for item in batch]
        values = lax.optimization_barrier(tuple(v for v, _ in todo) + first)
        came = [swap(v, mask) for v, (_, mask) in zip(values, todo)]
        held.update(zip(batch, came))
        for axis, name, j in batch:
            if axis == "x":
                if stack[0] is None:
                    stack[0] = jnp.zeros((half // 2, 2) + block.shape, BF16)
                placed.extend(j)
                for i, k in enumerate(j):
                    pair = slice(2 * i, 2 * i + 2)
                    stack[0] = put(stack[0], held["both", name, j][pair], place_own ^ k)
                    stack[0] = put(stack[0], held["x", name, j][pair], place_own ^ k ^ n_z)
                if len(placed) == n_z:
                    stack[0] = stack[0].reshape((half,) + block.shape)
        return tuple(came), values[len(batch) :]

    came, _ = run(rounds[0])

    ids, word_rows = after((caption_ids, word_table), came[-1])
    caption_count = caption_ids.shape[0]
    vocab_dev = word_table.shape[0]
    codes = me * vocab_dev + jnp.arange(vocab_dev, dtype=jnp.int32)
    counts = jnp.sum(ids[:, :, None] == codes[None, None, :], 1, dtype=F32).astype(BF16)
    words = dot(counts, word_rows, 1, 0)
    embed = words.shape[1]
    came, _ = run(rounds[1], *came)
    words = after(words, came[min(1, len(came) - 1)])
    words = lax.all_to_all(words.reshape(devices, -1, embed), BOTH, 0, 0)
    caption_own = jnp.sum(words, 0) / CAP_LEN

    t_in = after(jnp.concatenate([teacher_in, far_in], 0), came[-1])
    rows_t, t_width = teacher_in.shape
    own_rows = rows_t // n_grp
    t_rows = normalize_rows(t_in.astype(F32), teacher_gain).astype(BF16)
    came, _ = run(rounds[2], *came)

    own_in = after(pick(teacher_in, grp, own_rows), came[0])
    padded = n_chips * 4 * tile
    place = after(jnp.arange(padded, dtype=jnp.int32), came[0])
    canon = (((place // tile) ^ (4 * chip)) * n_head) + place % tile
    canon = jnp.where(place % tile < n_head, canon, -1)
    order = (jnp.arange(t_width, dtype=jnp.int32)[:, None] == canon[None, :]).astype(BF16)
    t_own = dot(own_in, lax.optimization_barrier(order), 1, 0, BF16)
    half_t = padded // 2
    s_rows = pick(after(student_in, came[0]), grp, own_rows).astype(F32)
    s_normed = normalize_rows(s_rows, student_gain).astype(BF16)
    came, (t_rows, caption_own, *_) = run(rounds[3], t_rows, caption_own, *came)

    ups = jnp.zeros((n_chips,) + up_pair.shape, BF16)
    came, (t_own, s_normed, *_) = run(rounds[4], t_own, s_normed, *came)
    for batch in rounds[5:-1]:
        came, _ = run(batch, *came)
    for k in range(n_z):
        ups = put(ups, held["z", "u", k], chip ^ (2 * k))
        ups = put(ups, held["y", "u", k], chip ^ (2 * k + 1))
    up_all = ups.reshape(t_width, half_w)
    t_act = gelu_tanh(dot(t_rows, up_all, 1, 0)).astype(BF16)
    far_stack = held["c", "s", 0]
    stack = stack[0]

    def rows_of(begin, size):
        part = [v[:, begin : begin + size].reshape(half * size, width) for v in (stack, far_stack)]
        return jnp.concatenate(part, 0)

    up_t = rows_of(0, n_up)
    down_w = rows_of(n_up, n_down)
    gate = dot(s_normed, up_t, 1, 1)
    s_act = gelu_tanh(gate).astype(BF16)
    s_out = s_rows + dot(s_act, down_w, 1, 0)
    s_round = s_out.astype(BF16)
    n_img = own_rows // PATCHES
    pooled = (jnp.sum(s_out.reshape(n_img, PATCHES, width), 1) / PATCHES).astype(BF16)
    sent = jnp.concatenate([pooled.astype(F32).reshape(-1), caption_own.reshape(-1)])

    def second(g):
        span = range(g * n_z // 2, (g + 1) * n_z // 2)
        return jnp.concatenate([w for k in span for w in (held["z", "d", k], held["y", "d", k])], 0)

    kept_rows = []

    def to_owner(g, down_g, far):
        part = (dot(t_act[:rows_t], down_g, 1, 1) + far.astype(F32)).astype(BF16)
        kept_rows.append(pick(part, grp, own_rows))
        return swap(pick(part, 1 - grp, own_rows), MASK_X)

    if n_z == 4:
        down_g = second(0)
        far = swap(dot(t_act[rows_t:], down_g, 1, 1, BF16), MASK_C)
        _, (far, sent, *_) = run(rounds[-1], far, sent, *came)
    else:
        _, (sent, *_) = run(rounds[-1], sent, *came)
        down_g = second(0)
        far = swap(dot(t_act[rows_t:], down_g, 1, 1, BF16), MASK_C)
    others = [to_owner(0, down_g, far)]
    got = lax.all_to_all(jnp.broadcast_to(sent[None], (devices,) + sent.shape), BOTH, 0, 0)

    begin = n_up + n_down + n_proj
    near_h, far_h = stack[:, begin:], after(far_stack, others[0])[:, begin:]
    heads = jnp.stack(
        [jnp.where(core == 0, near_h, far_h), jnp.where(core == 0, far_h, near_h)], 1
    )
    head_g = [heads[g * half // 2 : (g + 1) * half // 2].reshape(half_t, width) for g in range(2)]
    proj_rel = rows_of(n_up + n_down, n_proj)
    place_e = jnp.arange(devices * n_proj, dtype=jnp.int32)
    block_e = place_e // n_proj
    block_e = ((block_e % half) * 2 + ((block_e // half) ^ core)) ^ (4 * chip)
    from_e = block_e * n_proj + place_e % n_proj
    order_e = (place_e[:, None] == from_e[None, :]).astype(BF16)
    proj_t = dot(order_e, proj_rel, 1, 0, BF16)
    preds_s = [dot(s_round, head_g[g], 1, 1) for g in range(2)]

    pooled_all = got[:, : n_img * width].reshape(-1, width).astype(BF16)
    caption = unit_rows(got[:, n_img * width :].reshape(caption_count, embed))
    projected = dot(pooled_all, proj_t, 1, 1)
    proj_norm = jnp.sqrt(jnp.sum(projected * projected, -1, keepdims=True) + 1e-06)
    image = projected / proj_norm
    wanted = jnp.transpose(positive.reshape(n_dp, n_grp, n_img), (1, 0, 2)).reshape(-1)
    match = (wanted[:, None] == jnp.arange(caption_count, dtype=jnp.int32)[None, :]).astype(F32)
    scores = 100.0 * exact(image, caption, 1, 1)
    contrast = (
        jnp.sum(jax.nn.logsumexp(scores, 1))
        + jnp.sum(jax.nn.logsumexp(scores, 0))
        - 2.0 * jnp.sum(match * scores)
    )
    grad_scores = jax.nn.softmax(scores, 1) + jax.nn.softmax(scores, 0) - 2.0 * match
    grad_image = 100.0 * exact(grad_scores, caption, 1, 0)
    grad_projected = (
        (grad_image - image * jnp.sum(image * grad_image, -1, keepdims=True)) / proj_norm
    ).astype(BF16)
    grad_proj = dot(pick(grad_projected, me, n_proj, 1), pooled_all, 0, 0).T
    grad_pooled = dot(pick(grad_projected, me, n_img), proj_t, 1, 0) / PATCHES

    down_g = second(1)
    far = after(dot(t_act[rows_t:], down_g, 1, 1, BF16), others[0])
    others.append(to_owner(1, down_g, swap(far, MASK_C)))
    diffs = []
    for g in range(2):
        target = t_own[:, g * half_t : (g + 1) * half_t].astype(F32) + (
            kept_rows[g].astype(F32) + others[g].astype(F32)
        )
        diffs.append(preds_s[g] - target)
    feature = (jnp.sum(diffs[0] * diffs[0]) + jnp.sum(diffs[1] * diffs[1])) / t_width

    preds = [(2.0 * d / t_width).astype(BF16) for d in diffs]
    half_s = width // 2
    high = feature.astype(BF16).astype(F32)
    mid = (feature - high).astype(BF16).astype(F32)
    rest = feature - high - mid
    at = jnp.arange(width, dtype=jnp.int32)
    term = jnp.where(at % 3 == 0, high, jnp.where(at % 3 == 1, mid, rest))
    term = jnp.where(at // 3 == me, term, 0.0)
    spare = (jnp.arange(half_t, dtype=jnp.int32) % tile == n_head).astype(F32)[:, None]

    def head_part(pred, side):
        value = dot(pred, pick(s_round, side, half_s, 1), 0, 0)
        return value + spare * pick(term, side, half_s)[None, :]

    head_far = [queued(head_part(p, 1 - core).astype(BF16), MASK_C) for p in preds]
    head_parts = [head_part(p, core) + f.astype(F32) for p, f in zip(preds, head_far)]

    def take(sums, index, dim=0):
        return lax.dynamic_index_in_dim(sums, index, dim, False)

    def wide(values):
        return values.astype(F32)

    def flip_z(values, dim):
        shape = values.shape
        pairs = values.astype(BF16).reshape(shape[:dim] + (n_z // 2, 2) + shape[dim + 1 :])
        return jnp.flip(pairs, dim + 1).reshape(shape)

    def send_z(sums):
        if n_z == 4:
            both = jnp.stack([take(sums, z ^ 1 ^ low), take(sums, z ^ 2 ^ low)])
            return queued(both.astype(BF16), 4)
        return [queued(take(sums, z ^ k ^ low).astype(BF16), 4 * k) for k in range(1, n_z)]

    def add_z(sums, others):
        total = take(sums, z ^ low)
        if n_z == 4:
            far = take(sums, z ^ 3 ^ low) + wide(others[1])
            return total + wide(others[0]) + wide(queued(far.astype(BF16), 12))
        for other in others:
            total = total + wide(other)
        return total

    mine = (grp ^ top) == 0
    head_x = queued(jnp.where(mine, head_parts[1], head_parts[0]).astype(BF16), MASK_X)

    grad_out = dot(preds[0], head_g[0], 1, 0) + dot(preds[1], head_g[1], 1, 0)
    grad_out = (
        (grad_out.reshape(n_img, PATCHES, width) + grad_pooled[:, None, :])
        .reshape(-1, width)
        .astype(BF16)
    )

    part = s_act.shape[1] // 2
    down_far = queued(dot(s_act[:, part:], grad_out, 0, 0, BF16), MASK_C)
    grad_act = dot(grad_out, down_w, 1, 1)
    grad_gate = jax.vjp(gelu_tanh, gate)[1](grad_act)[0].astype(BF16)
    up_far = queued(dot(grad_gate[:, part:], s_normed, 0, 0, BF16), MASK_C)
    down = dot(s_act[:, :part], grad_out, 0, 0) + wide(down_far)
    up = dot(grad_gate[:, :part], s_normed, 0, 0) + wide(up_far)
    sums = [up.reshape(2, n_z, 2, n_up, width), down.reshape(2, n_z, 2, n_down, width)]

    def send(values, mask):
        return queued(jnp.concatenate([v.astype(BF16) for v in values], -2), mask)

    def add(values, came):
        return [values[0] + wide(came[..., :n_up, :]), values[1] + wide(came[..., n_up:, :])]

    hid_y = send([flip_z(take(v, 1 - y, 2), 1) for v in sums], MASK_Y)

    head = jnp.where(mine, head_parts[0], head_parts[1]) + wide(head_x)
    head = head.reshape(n_z, 2, 2, tile, half_s)
    head_z = send_z(head)

    sums = add([take(v, y, 2) for v in sums], hid_y)
    hid_x = send([take(v, (1 - grp) ^ top) for v in sums], MASK_X)

    head = add_z(head, head_z)
    head_y = queued(take(head, 1 - y).astype(BF16), MASK_Y)

    sums = add([take(v, grp ^ top) for v in sums], hid_x)
    if n_z == 4:
        near = [jnp.stack([take(v, z ^ 1 ^ low), take(v, z ^ 2 ^ low)]) for v in sums]
        hid_z = send(near, 4)
        far = add([take(v, z ^ 3 ^ low) for v in sums], hid_z[1])
        out = add([take(v, z ^ low) for v in sums], hid_z[0])
        hid_z = send(far, 12)

    head = take(head, y) + wide(head_y)
    kept = take(head, core)
    came = queued(take(head, 1 - core), MASK_C)
    head = jnp.where(
        core == 0, jnp.concatenate([kept, came], 1), jnp.concatenate([came, kept], 1)
    )
    grad_head = head[:n_head].T
    feature = jnp.sum(head[n_head])

    if n_z == 4:
        out = add(out, hid_z)
    else:
        out = [take(v, z ^ low) for v in sums]
        for k in range(1, n_z):
            out = add(out, send([take(v, z ^ k ^ low) for v in sums], 4 * k))
    grad_up, grad_down = out[0].T, out[1]

    loss = (feature + contrast) / (positive.shape[0] * PATCHES)
    return (loss, grad_up, grad_down, grad_head, grad_proj)


def solution(mesh):
    placed = (
        P("dp", None),
        P(),
        P("dp", "grp"),
        P("dp", "grp"),
        P("dp", None),
        P(),
        P(None, BOTH),
        P(BOTH, None),
        P(None, BOTH),
        P(None, BOTH),
        P(BOTH, None),
        P(),
        P(),
    )
    return jax.shard_map(
        local,
        mesh=mesh,
        in_specs=placed,
        out_specs=(
            P(),
            P(None, BOTH),
            P(BOTH, None),
            P(None, BOTH),
            P(None, BOTH),
        ),
        check_vma=False,
    )
```

```python
import jax
import jax.numpy as jnp
from jax import lax
from jax.sharding import PartitionSpec as P

CAP_LEN = 77
WINDOW = 7
PATCHES = 256
BOTH = ("grp", "dp")
BF16 = jnp.bfloat16
F32 = jnp.float32


def normalize_rows(values, gain):
    center = values - jnp.mean(values, -1, keepdims=True)
    spread = jnp.mean(center * center, -1, keepdims=True)
    return center * lax.rsqrt(spread + 1e-05) * gain


def gelu_tanh(values):
    return jax.nn.gelu(values, approximate=True)


def unit_rows(values):
    return values / jnp.sqrt(jnp.sum(values * values, -1, keepdims=True) + 1e-06)


def dot(a, b, ca, cb, out=F32):
    return lax.dot_general(a, b, (((ca,), (cb,)), ((), ())), preferred_element_type=F32).astype(out)


def exact(a, b, ca, cb):
    return lax.dot_general(
        a, b, (((ca,), (cb,)), ((), ())), precision=lax.Precision.HIGHEST, preferred_element_type=F32
    )


def pick(values, index, size, axis=0):
    return lax.dynamic_slice_in_dim(values, index * size, size, axis)


def after(values, *first):
    return lax.optimization_barrier((values,) + first)[0]


def local(
    teacher_in,
    teacher_gain,
    teacher_up,
    teacher_down,
    student_in,
    student_gain,
    student_up,
    student_down,
    student_head,
    student_proj,
    word_table,
    caption_ids,
    positive,
):
    grp = lax.axis_index("grp")
    dp = lax.axis_index("dp")
    n_grp = lax.axis_size("grp")
    n_dp = lax.axis_size("dp")
    devices = n_grp * n_dp
    n_z = n_dp // 4
    n_chips = n_dp // 2
    core = dp & 1
    chip = dp >> 1
    y = chip & 1
    z = chip >> 1
    me = grp * n_dp + dp
    MASK_C, MASK_Y, MASK_X = 1, 2, n_dp
    top = chip // n_z
    low = chip & (n_z - 1)
    even = chip - y
    low_even = even & (n_z - 1)

    def swap(values, mask):
        return lax.ppermute(values, BOTH, [(i, i ^ mask) for i in range(devices)])

    line = []

    def queued(values, mask, *first):
        first = first + tuple(line[: len(line) - WINDOW + 1][-6:] if len(line) >= WINDOW else ())
        if first:
            values = after(values, *first)
        line.append(swap(values, mask))
        return line[-1]

    def put(buffer, values, index):
        return lax.dynamic_update_slice(
            buffer, values[None], (index,) + (0,) * (buffer.ndim - 1)
        )

    width = student_in.shape[1]
    n_head = student_head.shape[1]
    tile = n_head + 8 - n_head % 8
    rows_w, hidden_w = teacher_up.shape
    half_w = hidden_w // 2
    at = jnp.arange(2 * tile, dtype=jnp.int32)
    at = jnp.where(at % tile < n_head, (at // tile) * n_head + at % tile, -1)
    widen = (at[:, None] == jnp.arange(rows_w, dtype=jnp.int32)[None, :]).astype(BF16)
    send_up = pick(teacher_up, 1 - core, half_w, 1)
    down_rows = lax.optimization_barrier(dot(widen, teacher_down, 1, 0, BF16))
    send_down = pick(down_rows, 1 - core, half_w, 1)
    far_up, far_down, far_in = swap(send_up, MASK_C), swap(send_down, MASK_C), swap(teacher_in, MASK_C)
    own_up = pick(teacher_up, core, half_w, 1)
    own_down = pick(down_rows, core, half_w, 1)

    def in_order(mine, other):
        return jnp.stack([jnp.where(core == 0, mine, other), jnp.where(core == 0, other, mine)])

    up_pair = in_order(own_up, far_up).reshape(2 * rows_w, half_w)
    down_pair = in_order(own_down, far_down).reshape(4 * tile, half_w)

    n_up = student_up.shape[1]
    n_down = student_down.shape[0]
    n_proj = student_proj.shape[1]
    head_rows = dot(widen[:tile, :n_head], student_head, 1, 1, BF16)
    block = jnp.concatenate(
        [
            after(student_up, send_up, send_down).T,
            student_down,
            student_proj.T,
            head_rows,
        ],
        0,
    )

    half = devices // 2
    place_own = (me ^ (4 * even)) >> 2
    if n_z == 4:
        rounds = [
            [("z", "s", 3), ("z", "s", 1), ("y", "s", 0), ("y", "u", 0)],
            [("z", "u", 3), ("z", "s", 2), ("y", "s", 3), ("y", "s", 1), ("x", "s", (0,))],
            [("zz", "u", 1), ("y", "s", 2), ("y", "u", 3), ("x", "s", (1, 3)), ("y", "d", 0)],
            [("z", "d", 3), ("z", "d", 1), ("y", "u", 1), ("y", "u", 2), ("x", "s", (2,))],
            [("c", "s", 0), ("z", "d", 2), ("y", "d", 1), ("y", "d", 3)],
            [("y", "d", 2)],
        ]
    else:
        some = [("z", p, j) for p in "sud" for j in range(1, n_z)]
        some += [("y", p, j) for p in "sud" for j in range(n_z)]
        some += [("x", "s", (j,)) for j in range(n_z)] + [("c", "s", 0)]
        some += [some.pop(some.index(("y", "d", n_z - 1)))]
        rounds = [some[i : i + 1] for i in range(len(some))]
    held = {("z", "s", 0): block, ("z", "u", 0): up_pair, ("z", "d", 0): down_pair}
    stack, placed = [None], []

    def values_of(axis, name, j):
        if axis == "zz":
            return jnp.stack([held["z", name, 0], held["z", name, 3]]), 4
        if axis == "z" and n_z == 4 and j == 2:
            return held["z", name, 3], 4
        if axis == "z":
            return held["z", name, 0], 4 * j
        if axis == "y":
            return held["z", name, j], MASK_Y
        if axis == "x":
            both = []
            for k in j:
                mine, theirs = held["z", name, k], held["y", name, k]
                both += [jnp.where(y == 0, mine, theirs), jnp.where(y == 0, theirs, mine)]
            held["both", name, j] = jnp.stack(both)
            return held["both", name, j], MASK_X
        return stack[0], MASK_C

    def run(batch, *first):
        todo = [values_of(*item) for item in batch]
        values = lax.optimization_barrier(tuple(v for v, _ in todo) + first)
        came = [swap(v, mask) for v, (_, mask) in zip(values, todo)]
        held.update(zip(batch, came))
        for axis, name, j in batch:
            if axis == "zz":
                held["z", name, 1], held["z", name, 2] = held[axis, name, j]
            if axis == "x":
                if stack[0] is None:
                    stack[0] = jnp.zeros((half // 2, 2) + block.shape, BF16)
                placed.extend(j)
                for i, k in enumerate(j):
                    pair = slice(2 * i, 2 * i + 2)
                    stack[0] = put(stack[0], held["both", name, j][pair], place_own ^ k)
                    stack[0] = put(stack[0], held["x", name, j][pair], place_own ^ k ^ n_z)
                if len(placed) == n_z:
                    stack[0] = stack[0].reshape((half,) + block.shape)
        return tuple(came), values[len(batch) :]

    came, _ = run(rounds[0])

    ids, word_rows = after((caption_ids, word_table), came[-1])
    caption_count = caption_ids.shape[0]
    vocab_dev = word_table.shape[0]
    codes = me * vocab_dev + jnp.arange(vocab_dev, dtype=jnp.int32)
    counts = jnp.sum(ids[:, :, None] == codes[None, None, :], 1, dtype=F32).astype(BF16)
    words = dot(counts, word_rows, 1, 0)
    embed = words.shape[1]
    came, _ = run(rounds[1], *came)
    words = after(words, came[min(1, len(came) - 1)])
    words = lax.all_to_all(words.reshape(devices, -1, embed), BOTH, 0, 0)
    caption_own = jnp.sum(words, 0) / CAP_LEN

    t_in = after(jnp.concatenate([teacher_in, far_in], 0), came[-1])
    rows_t, t_width = teacher_in.shape
    own_rows = rows_t // n_grp
    t_rows = normalize_rows(t_in.astype(F32), teacher_gain).astype(BF16)
    came, _ = run(rounds[2], *came)

    own_in = after(pick(teacher_in, grp, own_rows), came[0])
    padded = n_chips * 4 * tile
    place = after(jnp.arange(padded, dtype=jnp.int32), came[0])
    canon = (((place // tile) ^ (4 * chip)) * n_head) + place % tile
    canon = jnp.where(place % tile < n_head, canon, -1)
    order = (jnp.arange(t_width, dtype=jnp.int32)[:, None] == canon[None, :]).astype(BF16)
    t_own = dot(own_in, lax.optimization_barrier(order), 1, 0, BF16)
    half_t = padded // 2
    s_rows = pick(after(student_in, came[0]), grp, own_rows).astype(F32)
    s_normed = normalize_rows(s_rows, student_gain).astype(BF16)
    came, (t_rows, caption_own, *_) = run(rounds[3], t_rows, caption_own, *came)

    ups = jnp.zeros((n_chips,) + up_pair.shape, BF16)
    came, (t_own, s_normed, *_) = run(rounds[4], t_own, s_normed, *came)
    for batch in rounds[5:-1]:
        came, _ = run(batch, *came)
    for k in range(n_z):
        ups = put(ups, held["z", "u", k], chip ^ (2 * k))
        ups = put(ups, held["y", "u", k], chip ^ (2 * k + 1))
    up_all = ups.reshape(t_width, half_w)
    t_act = gelu_tanh(dot(t_rows, up_all, 1, 0)).astype(BF16)
    far_stack = held["c", "s", 0]
    stack = stack[0]

    def rows_of(begin, size):
        part = [v[:, begin : begin + size].reshape(half * size, width) for v in (stack, far_stack)]
        return jnp.concatenate(part, 0)

    up_t = rows_of(0, n_up)
    down_w = rows_of(n_up, n_down)
    gate = dot(s_normed, up_t, 1, 1)
    s_act = gelu_tanh(gate).astype(BF16)
    s_out = s_rows + dot(s_act, down_w, 1, 0)
    s_round = s_out.astype(BF16)
    n_img = own_rows // PATCHES
    pooled = (jnp.sum(s_out.reshape(n_img, PATCHES, width), 1) / PATCHES).astype(BF16)
    sent = jnp.concatenate([pooled.astype(F32).reshape(-1), caption_own.reshape(-1)])

    def second(g):
        span = range(g * n_z // 2, (g + 1) * n_z // 2)
        return jnp.concatenate([w for k in span for w in (held["z", "d", k], held["y", "d", k])], 0)

    kept_rows = []

    def to_owner(g, down_g, far):
        part = (dot(t_act[:rows_t], down_g, 1, 1) + far.astype(F32)).astype(BF16)
        kept_rows.append(pick(part, grp, own_rows))
        return swap(pick(part, 1 - grp, own_rows), MASK_X)

    if n_z == 4:
        down_g = second(0)
        far = swap(dot(t_act[rows_t:], down_g, 1, 1, BF16), MASK_C)
        _, (far, sent, *_) = run(rounds[-1], far, sent, *came)
    else:
        _, (sent, *_) = run(rounds[-1], sent, *came)
        down_g = second(0)
        far = swap(dot(t_act[rows_t:], down_g, 1, 1, BF16), MASK_C)
    others = [to_owner(0, down_g, far)]
    got = lax.all_to_all(jnp.broadcast_to(sent[None], (devices,) + sent.shape), BOTH, 0, 0)

    begin = n_up + n_down + n_proj
    near_h, far_h = stack[:, begin:], after(far_stack, others[0])[:, begin:]
    heads = jnp.stack(
        [jnp.where(core == 0, near_h, far_h), jnp.where(core == 0, far_h, near_h)], 1
    )
    heads = heads.reshape((n_chips // 2, 2, 2) + heads.shape[1:])
    heads = jnp.stack(
        [jnp.where(y == 0, heads[:, i], heads[:, 1 - i]) for i in range(2)], 1
    ).reshape((half,) + heads.shape[3:])
    head_g = [heads[g * half // 2 : (g + 1) * half // 2].reshape(half_t, width) for g in range(2)]
    proj_rel = rows_of(n_up + n_down, n_proj)
    place_e = jnp.arange(devices * n_proj, dtype=jnp.int32)
    block_e = place_e // n_proj
    block_e = ((block_e % half) * 2 + ((block_e // half) ^ core)) ^ (4 * even)
    from_e = block_e * n_proj + place_e % n_proj
    order_e = (place_e[:, None] == from_e[None, :]).astype(BF16)
    proj_t = dot(order_e, proj_rel, 1, 0, BF16)
    preds_s = [dot(s_round, head_g[g], 1, 1) for g in range(2)]

    pooled_all = got[:, : n_img * width].reshape(-1, width).astype(BF16)
    caption = unit_rows(got[:, n_img * width :].reshape(caption_count, embed))
    projected = dot(pooled_all, proj_t, 1, 1)
    proj_norm = jnp.sqrt(jnp.sum(projected * projected, -1, keepdims=True) + 1e-06)
    image = projected / proj_norm
    wanted = jnp.transpose(positive.reshape(n_dp, n_grp, n_img), (1, 0, 2)).reshape(-1)
    match = (wanted[:, None] == jnp.arange(caption_count, dtype=jnp.int32)[None, :]).astype(F32)
    scores = 100.0 * exact(image, caption, 1, 1)
    contrast = (
        jnp.sum(jax.nn.logsumexp(scores, 1))
        + jnp.sum(jax.nn.logsumexp(scores, 0))
        - 2.0 * jnp.sum(match * scores)
    )
    grad_scores = jax.nn.softmax(scores, 1) + jax.nn.softmax(scores, 0) - 2.0 * match
    grad_image = 100.0 * exact(grad_scores, caption, 1, 0)
    grad_projected = (
        (grad_image - image * jnp.sum(image * grad_image, -1, keepdims=True)) / proj_norm
    ).astype(BF16)
    grad_proj = dot(pick(grad_projected, me, n_proj, 1), pooled_all, 0, 0).T
    grad_pooled = dot(pick(grad_projected, me, n_img), proj_t, 1, 0) / PATCHES

    down_g = second(1)
    far = after(dot(t_act[rows_t:], down_g, 1, 1, BF16), others[0])
    others.append(to_owner(1, down_g, swap(far, MASK_C)))
    diffs = []
    for g in range(2):
        target = t_own[:, g * half_t : (g + 1) * half_t].astype(F32) + (
            kept_rows[g].astype(F32) + others[g].astype(F32)
        )
        diffs.append(preds_s[g] - target)
    feature = (jnp.sum(diffs[0] * diffs[0]) + jnp.sum(diffs[1] * diffs[1])) / t_width

    preds = [(2.0 * d / t_width).astype(BF16) for d in diffs]
    half_s = width // 2
    high = feature.astype(BF16).astype(F32)
    mid = (feature - high).astype(BF16).astype(F32)
    rest = feature - high - mid
    at = jnp.arange(width, dtype=jnp.int32)
    term = jnp.where(at % 3 == 0, high, jnp.where(at % 3 == 1, mid, rest))
    term = jnp.where(at // 3 == me, term, 0.0)
    spare = (jnp.arange(half_t, dtype=jnp.int32) % tile == n_head).astype(F32)[:, None]

    def head_part(pred, side):
        value = dot(pred, pick(s_round, side, half_s, 1), 0, 0)
        return value + spare * pick(term, side, half_s)[None, :]

    head_far = [queued(head_part(p, 1 - core).astype(BF16), MASK_C) for p in preds]
    head_parts = [head_part(p, core) + f.astype(F32) for p, f in zip(preds, head_far)]

    def take(sums, index, dim=0):
        return lax.dynamic_index_in_dim(sums, index, dim, False)

    def wide(values):
        return values.astype(F32)

    def send_z(sums):
        if n_z == 4:
            both = jnp.stack([take(sums, z ^ 1 ^ low), take(sums, z ^ 2 ^ low)])
            return queued(both.astype(BF16), 4)
        return [queued(take(sums, z ^ k ^ low).astype(BF16), 4 * k) for k in range(1, n_z)]

    def add_z(sums, others):
        total = take(sums, z ^ low)
        if n_z == 4:
            far = take(sums, z ^ 3 ^ low) + wide(others[1])
            return total + wide(others[0]) + wide(queued(far.astype(BF16), 12))
        for other in others:
            total = total + wide(other)
        return total

    mine = (grp ^ top) == 0
    head_x = queued(jnp.where(mine, head_parts[1], head_parts[0]).astype(BF16), MASK_X)

    grad_out = dot(preds[0], head_g[0], 1, 0) + dot(preds[1], head_g[1], 1, 0)
    grad_out = (
        (grad_out.reshape(n_img, PATCHES, width) + grad_pooled[:, None, :])
        .reshape(-1, width)
        .astype(BF16)
    )

    part = s_act.shape[1] // 2
    down_far = queued(dot(s_act[:, part:], grad_out, 0, 0, BF16), MASK_C)
    grad_act = dot(grad_out, down_w, 1, 1)
    grad_gate = jax.vjp(gelu_tanh, gate)[1](grad_act)[0].astype(BF16)
    up_far = queued(dot(grad_gate[:, part:], s_normed, 0, 0, BF16), MASK_C)
    down = dot(s_act[:, :part], grad_out, 0, 0) + wide(down_far)
    up = dot(grad_gate[:, :part], s_normed, 0, 0) + wide(up_far)
    sums = [up.reshape(2, n_z, 2, n_up, width), down.reshape(2, n_z, 2, n_down, width)]

    def send(values, mask):
        return queued(jnp.concatenate([v.astype(BF16) for v in values], -2), mask)

    def add(values, came):
        return [values[0] + wide(came[..., :n_up, :]), values[1] + wide(came[..., n_up:, :])]

    hid_y = send([take(v, 1 - y, 2) for v in sums], MASK_Y)

    head = jnp.where(mine, head_parts[0], head_parts[1]) + wide(head_x)
    head = head.reshape(n_z, 2, 2, tile, half_s)
    head_z = send_z(head)

    sums = add([take(v, y, 2) for v in sums], hid_y)
    hid_x = send([take(v, (1 - grp) ^ top) for v in sums], MASK_X)

    head = add_z(head, head_z)
    head_y = queued(take(head, 1 - y).astype(BF16), MASK_Y)

    sums = add([take(v, grp ^ top) for v in sums], hid_x)
    if n_z == 4:
        near = [jnp.stack([take(v, z ^ 1 ^ low_even), take(v, z ^ 2 ^ low_even)]) for v in sums]
        hid_z = send(near, 4)
        far = add([take(v, z ^ 3 ^ low_even) for v in sums], hid_z[1])
        out = add([take(v, z ^ low_even) for v in sums], hid_z[0])
        hid_z = send(far, 12)

    head = take(head, y) + wide(head_y)
    kept = take(head, core)
    came = queued(take(head, 1 - core), MASK_C)
    head = jnp.where(
        core == 0, jnp.concatenate([kept, came], 1), jnp.concatenate([came, kept], 1)
    )
    grad_head = head[:n_head].T
    feature = jnp.sum(head[n_head])

    if n_z == 4:
        out = add(out, hid_z)
    else:
        out = [take(v, z ^ low_even) for v in sums]
        for k in range(1, n_z):
            out = add(out, send([take(v, z ^ k ^ low_even) for v in sums], 4 * k))
    grad_up, grad_down = out[0].T, out[1]

    loss = (feature + contrast) / (positive.shape[0] * PATCHES)
    return (loss, grad_up, grad_down, grad_head, grad_proj)


def solution(mesh):
    placed = (
        P("dp", None),
        P(),
        P("dp", "grp"),
        P("dp", "grp"),
        P("dp", None),
        P(),
        P(None, BOTH),
        P(BOTH, None),
        P(None, BOTH),
        P(None, BOTH),
        P(BOTH, None),
        P(),
        P(),
    )
    return jax.shard_map(
        local,
        mesh=mesh,
        in_specs=placed,
        out_specs=(
            P(),
            P(None, BOTH),
            P(BOTH, None),
            P(None, BOTH),
            P(None, BOTH),
        ),
        check_vma=False,
    )
```

```python
import jax
import jax.numpy as jnp
from jax import lax
from jax.sharding import PartitionSpec as P

CAP_LEN = 77
WINDOW = 7
PATCHES = 256
BOTH = ("grp", "dp")
BF16 = jnp.bfloat16
F32 = jnp.float32


def normalize_rows(values, gain):
    center = values - jnp.mean(values, -1, keepdims=True)
    spread = jnp.mean(center * center, -1, keepdims=True)
    return center * lax.rsqrt(spread + 1e-05) * gain


def gelu_tanh(values):
    return jax.nn.gelu(values, approximate=True)


def unit_rows(values):
    return values / jnp.sqrt(jnp.sum(values * values, -1, keepdims=True) + 1e-06)


def dot(a, b, ca, cb, out=F32):
    return lax.dot_general(a, b, (((ca,), (cb,)), ((), ())), preferred_element_type=F32).astype(out)


def exact(a, b, ca, cb):
    return lax.dot_general(
        a, b, (((ca,), (cb,)), ((), ())), precision=lax.Precision.HIGHEST, preferred_element_type=F32
    )


def pick(values, index, size, axis=0):
    return lax.dynamic_slice_in_dim(values, index * size, size, axis)


def after(values, *first):
    return lax.optimization_barrier((values,) + first)[0]


def local(
    teacher_in,
    teacher_gain,
    teacher_up,
    teacher_down,
    student_in,
    student_gain,
    student_up,
    student_down,
    student_head,
    student_proj,
    word_table,
    caption_ids,
    positive,
):
    grp = lax.axis_index("grp")
    dp = lax.axis_index("dp")
    n_grp = lax.axis_size("grp")
    n_dp = lax.axis_size("dp")
    devices = n_grp * n_dp
    n_z = n_dp // 4
    n_chips = n_dp // 2
    core = dp & 1
    chip = dp >> 1
    y = chip & 1
    z = chip >> 1
    me = grp * n_dp + dp
    MASK_C, MASK_Y, MASK_X = 1, 2, n_dp
    top = chip // n_z
    low = chip & (n_z - 1)
    even = chip - y
    low_even = even & (n_z - 1)

    def swap(values, mask):
        return lax.ppermute(values, BOTH, [(i, i ^ mask) for i in range(devices)])

    line = []

    def queued(values, mask, *first):
        first = first + tuple(line[: len(line) - WINDOW + 1][-6:] if len(line) >= WINDOW else ())
        if first:
            values = after(values, *first)
        line.append(swap(values, mask))
        return line[-1]

    def put(buffer, values, index):
        return lax.dynamic_update_slice(
            buffer, values[None], (index,) + (0,) * (buffer.ndim - 1)
        )

    width = student_in.shape[1]
    n_head = student_head.shape[1]
    tile = n_head + 8 - n_head % 8
    rows_w, hidden_w = teacher_up.shape
    half_w = hidden_w // 2
    at = jnp.arange(2 * tile, dtype=jnp.int32)
    at = jnp.where(at % tile < n_head, (at // tile) * n_head + at % tile, -1)
    widen = (at[:, None] == jnp.arange(rows_w, dtype=jnp.int32)[None, :]).astype(BF16)
    send_up = pick(teacher_up, 1 - core, half_w, 1)
    down_rows = lax.optimization_barrier(dot(widen, teacher_down, 1, 0, BF16))
    send_down = pick(down_rows, 1 - core, half_w, 1)
    far_up, far_down, far_in = swap(send_up, MASK_C), swap(send_down, MASK_C), swap(teacher_in, MASK_C)
    own_up = pick(teacher_up, core, half_w, 1)
    own_down = pick(down_rows, core, half_w, 1)

    def in_order(mine, other):
        return jnp.stack([jnp.where(core == 0, mine, other), jnp.where(core == 0, other, mine)])

    up_pair = in_order(own_up, far_up).reshape(2 * rows_w, half_w)
    down_pair = in_order(own_down, far_down).reshape(4 * tile, half_w)

    n_up = student_up.shape[1]
    n_down = student_down.shape[0]
    n_proj = student_proj.shape[1]
    head_rows = dot(widen[:tile, :n_head], student_head, 1, 1, BF16)
    block = jnp.concatenate(
        [
            after(student_up, send_up, send_down).T,
            student_down,
            student_proj.T,
            head_rows,
        ],
        0,
    )

    half = devices // 2
    place_own = (me ^ (4 * even)) >> 2
    if n_z == 4:
        rounds = [
            [("z", "s", 3), ("z", "s", 1), ("y", "s", 0), ("y", "u", 0)],
            [("z", "u", 3), ("z", "s", 2), ("y", "s", 3), ("y", "s", 1), ("x", "s", (0,))],
            [("zz", "u", 1), ("y", "s", 2), ("y", "u", 3), ("x", "s", (1, 3)), ("y", "d", 0)],
            [("z", "d", 3), ("z", "d", 1), ("yy", "u", 1), ("x", "s", (2,))],
            [("c", "s", 0), ("z", "d", 2), ("y", "d", 1), ("y", "d", 3)],
            [("y", "d", 2)],
        ]
    else:
        some = [("z", p, j) for p in "sud" for j in range(1, n_z)]
        some += [("y", p, j) for p in "sud" for j in range(n_z)]
        some += [("x", "s", (j,)) for j in range(n_z)] + [("c", "s", 0)]
        some += [some.pop(some.index(("y", "d", n_z - 1)))]
        rounds = [some[i : i + 1] for i in range(len(some))]
    held = {("z", "s", 0): block, ("z", "u", 0): up_pair, ("z", "d", 0): down_pair}
    stack, placed = [None], []

    def values_of(axis, name, j):
        if axis == "yy":
            return held["zz", name, j], MASK_Y
        if axis == "zz":
            return jnp.stack([held["z", name, 0], held["z", name, 3]]), 4
        if axis == "z" and n_z == 4 and j == 2:
            return held["z", name, 3], 4
        if axis == "z":
            return held["z", name, 0], 4 * j
        if axis == "y":
            return held["z", name, j], MASK_Y
        if axis == "x":
            both = []
            for k in j:
                mine, theirs = held["z", name, k], held["y", name, k]
                both += [jnp.where(y == 0, mine, theirs), jnp.where(y == 0, theirs, mine)]
            held["both", name, j] = jnp.stack(both)
            return held["both", name, j], MASK_X
        return stack[0], MASK_C

    def run(batch, *first):
        todo = [values_of(*item) for item in batch]
        values = lax.optimization_barrier(tuple(v for v, _ in todo) + first)
        came = [swap(v, mask) for v, (_, mask) in zip(values, todo)]
        held.update(zip(batch, came))
        for axis, name, j in batch:
            if axis == "yy":
                held["y", name, 1], held["y", name, 2] = held[axis, name, j]
            if axis == "zz":
                held["z", name, 1], held["z", name, 2] = held[axis, name, j]
            if axis == "x":
                if stack[0] is None:
                    stack[0] = jnp.zeros((half // 2, 2) + block.shape, BF16)
                placed.extend(j)
                for i, k in enumerate(j):
                    pair = slice(2 * i, 2 * i + 2)
                    stack[0] = put(stack[0], held["both", name, j][pair], place_own ^ k)
                    stack[0] = put(stack[0], held["x", name, j][pair], place_own ^ k ^ n_z)
                if len(placed) == n_z:
                    stack[0] = stack[0].reshape((half,) + block.shape)
        return tuple(came), values[len(batch) :]

    came, _ = run(rounds[0])

    ids, word_rows = after((caption_ids, word_table), came[-1])
    caption_count = caption_ids.shape[0]
    vocab_dev = word_table.shape[0]
    codes = me * vocab_dev + jnp.arange(vocab_dev, dtype=jnp.int32)
    counts = jnp.sum(ids[:, :, None] == codes[None, None, :], 1, dtype=F32).astype(BF16)
    words = dot(counts, word_rows, 1, 0)
    embed = words.shape[1]
    came, _ = run(rounds[1], *came)
    words = after(words, came[min(1, len(came) - 1)])
    words = lax.all_to_all(words.reshape(devices, -1, embed), BOTH, 0, 0)
    caption_own = jnp.sum(words, 0) / CAP_LEN

    t_in = after(jnp.concatenate([teacher_in, far_in], 0), came[-1])
    rows_t, t_width = teacher_in.shape
    own_rows = rows_t // n_grp
    t_rows = normalize_rows(t_in.astype(F32), teacher_gain).astype(BF16)
    came, _ = run(rounds[2], *came)

    own_in = after(pick(teacher_in, grp, own_rows), came[0])
    padded = n_chips * 4 * tile
    place = after(jnp.arange(padded, dtype=jnp.int32), came[0])
    canon = (((place // tile) ^ (4 * chip)) * n_head) + place % tile
    canon = jnp.where(place % tile < n_head, canon, -1)
    order = (jnp.arange(t_width, dtype=jnp.int32)[:, None] == canon[None, :]).astype(BF16)
    t_own = dot(own_in, lax.optimization_barrier(order), 1, 0, BF16)
    half_t = padded // 2
    s_rows = pick(after(student_in, came[0]), grp, own_rows).astype(F32)
    s_normed = normalize_rows(s_rows, student_gain).astype(BF16)
    came, (t_rows, caption_own, *_) = run(rounds[3], t_rows, caption_own, *came)

    ups = jnp.zeros((n_chips,) + up_pair.shape, BF16)
    came, (t_own, s_normed, *_) = run(rounds[4], t_own, s_normed, *came)
    for batch in rounds[5:-1]:
        came, _ = run(batch, *came)
    for k in range(n_z):
        ups = put(ups, held["z", "u", k], chip ^ (2 * k))
        ups = put(ups, held["y", "u", k], chip ^ (2 * k + 1))
    up_all = ups.reshape(t_width, half_w)
    t_act = gelu_tanh(dot(t_rows, up_all, 1, 0)).astype(BF16)
    far_stack = held["c", "s", 0]
    stack = stack[0]

    def rows_of(begin, size):
        part = [v[:, begin : begin + size].reshape(half * size, width) for v in (stack, far_stack)]
        return jnp.concatenate(part, 0)

    up_t = rows_of(0, n_up)
    down_w = rows_of(n_up, n_down)
    gate = dot(s_normed, up_t, 1, 1)
    s_act = gelu_tanh(gate).astype(BF16)
    s_out = s_rows + dot(s_act, down_w, 1, 0)
    s_round = s_out.astype(BF16)
    n_img = own_rows // PATCHES
    pooled = (jnp.sum(s_out.reshape(n_img, PATCHES, width), 1) / PATCHES).astype(BF16)
    sent = jnp.concatenate([pooled.astype(F32).reshape(-1), caption_own.reshape(-1)])

    def second(g):
        span = range(g * n_z // 2, (g + 1) * n_z // 2)
        return jnp.concatenate([w for k in span for w in (held["z", "d", k], held["y", "d", k])], 0)

    kept_rows = []

    def to_owner(g, down_g, far):
        part = (dot(t_act[:rows_t], down_g, 1, 1) + far.astype(F32)).astype(BF16)
        kept_rows.append(pick(part, grp, own_rows))
        return swap(pick(part, 1 - grp, own_rows), MASK_X)

    if n_z == 4:
        down_g = second(0)
        far = swap(dot(t_act[rows_t:], down_g, 1, 1, BF16), MASK_C)
        _, (far, sent, *_) = run(rounds[-1], far, sent, *came)
    else:
        _, (sent, *_) = run(rounds[-1], sent, *came)
        down_g = second(0)
        far = swap(dot(t_act[rows_t:], down_g, 1, 1, BF16), MASK_C)
    others = [to_owner(0, down_g, far)]
    got = lax.all_to_all(jnp.broadcast_to(sent[None], (devices,) + sent.shape), BOTH, 0, 0)

    begin = n_up + n_down + n_proj
    near_h, far_h = stack[:, begin:], after(far_stack, others[0])[:, begin:]
    heads = jnp.stack(
        [jnp.where(core == 0, near_h, far_h), jnp.where(core == 0, far_h, near_h)], 1
    )
    heads = heads.reshape((n_chips // 2, 2, 2) + heads.shape[1:])
    heads = jnp.stack(
        [jnp.where(y == 0, heads[:, i], heads[:, 1 - i]) for i in range(2)], 1
    ).reshape((half,) + heads.shape[3:])
    head_g = [heads[g * half // 2 : (g + 1) * half // 2].reshape(half_t, width) for g in range(2)]
    proj_rel = rows_of(n_up + n_down, n_proj)
    place_e = jnp.arange(devices * n_proj, dtype=jnp.int32)
    block_e = place_e // n_proj
    block_e = ((block_e % half) * 2 + ((block_e // half) ^ core)) ^ (4 * even)
    from_e = block_e * n_proj + place_e % n_proj
    order_e = (place_e[:, None] == from_e[None, :]).astype(BF16)
    proj_t = dot(order_e, proj_rel, 1, 0, BF16)
    preds_s = [dot(s_round, head_g[g], 1, 1) for g in range(2)]

    pooled_all = got[:, : n_img * width].reshape(-1, width).astype(BF16)
    caption = unit_rows(got[:, n_img * width :].reshape(caption_count, embed))
    projected = dot(pooled_all, proj_t, 1, 1)
    proj_norm = jnp.sqrt(jnp.sum(projected * projected, -1, keepdims=True) + 1e-06)
    image = projected / proj_norm
    wanted = jnp.transpose(positive.reshape(n_dp, n_grp, n_img), (1, 0, 2)).reshape(-1)
    match = (wanted[:, None] == jnp.arange(caption_count, dtype=jnp.int32)[None, :]).astype(F32)
    scores = 100.0 * exact(image, caption, 1, 1)
    contrast = (
        jnp.sum(jax.nn.logsumexp(scores, 1))
        + jnp.sum(jax.nn.logsumexp(scores, 0))
        - 2.0 * jnp.sum(match * scores)
    )
    grad_scores = jax.nn.softmax(scores, 1) + jax.nn.softmax(scores, 0) - 2.0 * match
    grad_image = 100.0 * exact(grad_scores, caption, 1, 0)
    grad_projected = (
        (grad_image - image * jnp.sum(image * grad_image, -1, keepdims=True)) / proj_norm
    ).astype(BF16)
    grad_proj = dot(pick(grad_projected, me, n_proj, 1), pooled_all, 0, 0).T
    grad_pooled = dot(pick(grad_projected, me, n_img), proj_t, 1, 0) / PATCHES

    down_g = second(1)
    far = after(dot(t_act[rows_t:], down_g, 1, 1, BF16), others[0])
    others.append(to_owner(1, down_g, swap(far, MASK_C)))
    diffs = []
    for g in range(2):
        target = t_own[:, g * half_t : (g + 1) * half_t].astype(F32) + (
            kept_rows[g].astype(F32) + others[g].astype(F32)
        )
        diffs.append(preds_s[g] - target)
    feature = (jnp.sum(diffs[0] * diffs[0]) + jnp.sum(diffs[1] * diffs[1])) / t_width

    preds = [(2.0 * d / t_width).astype(BF16) for d in diffs]
    half_s = width // 2
    high = feature.astype(BF16).astype(F32)
    mid = (feature - high).astype(BF16).astype(F32)
    rest = feature - high - mid
    at = jnp.arange(width, dtype=jnp.int32)
    term = jnp.where(at % 3 == 0, high, jnp.where(at % 3 == 1, mid, rest))
    term = jnp.where(at // 3 == me, term, 0.0)
    spare = (jnp.arange(half_t, dtype=jnp.int32) % tile == n_head).astype(F32)[:, None]

    def head_part(pred, side):
        value = dot(pred, pick(s_round, side, half_s, 1), 0, 0)
        return value + spare * pick(term, side, half_s)[None, :]

    head_far = [queued(head_part(p, 1 - core).astype(BF16), MASK_C) for p in preds]
    head_parts = [head_part(p, core) + f.astype(F32) for p, f in zip(preds, head_far)]

    def take(sums, index, dim=0):
        return lax.dynamic_index_in_dim(sums, index, dim, False)

    def wide(values):
        return values.astype(F32)

    def send_z(sums):
        if n_z == 4:
            both = jnp.stack([take(sums, z ^ 1 ^ low), take(sums, z ^ 2 ^ low)])
            return queued(both.astype(BF16), 4)
        return [queued(take(sums, z ^ k ^ low).astype(BF16), 4 * k) for k in range(1, n_z)]

    def add_z(sums, others):
        total = take(sums, z ^ low)
        if n_z == 4:
            far = take(sums, z ^ 3 ^ low) + wide(others[1])
            return total + wide(others[0]) + wide(queued(far.astype(BF16), 12))
        for other in others:
            total = total + wide(other)
        return total

    mine = (grp ^ top) == 0
    head_x = queued(jnp.where(mine, head_parts[1], head_parts[0]).astype(BF16), MASK_X)

    grad_out = dot(preds[0], head_g[0], 1, 0) + dot(preds[1], head_g[1], 1, 0)
    grad_out = (
        (grad_out.reshape(n_img, PATCHES, width) + grad_pooled[:, None, :])
        .reshape(-1, width)
        .astype(BF16)
    )

    part = s_act.shape[1] // 2
    down_far = queued(dot(s_act[:, part:], grad_out, 0, 0, BF16), MASK_C)
    grad_act = dot(grad_out, down_w, 1, 1)
    grad_gate = jax.vjp(gelu_tanh, gate)[1](grad_act)[0].astype(BF16)
    up_far = queued(dot(grad_gate[:, part:], s_normed, 0, 0, BF16), MASK_C)
    down = dot(s_act[:, :part], grad_out, 0, 0) + wide(down_far)
    up = dot(grad_gate[:, :part], s_normed, 0, 0) + wide(up_far)
    sums = [up.reshape(2, n_z, 2, n_up, width), down.reshape(2, n_z, 2, n_down, width)]

    def send(values, mask):
        return queued(jnp.concatenate([v.astype(BF16) for v in values], -2), mask)

    def add(values, came):
        return [values[0] + wide(came[..., :n_up, :]), values[1] + wide(came[..., n_up:, :])]

    hid_y = send([take(v, 1 - y, 2) for v in sums], MASK_Y)

    head = jnp.where(mine, head_parts[0], head_parts[1]) + wide(head_x)
    head = head.reshape(n_z, 2, 2, tile, half_s)
    head_z = send_z(head)

    sums = add([take(v, y, 2) for v in sums], hid_y)
    hid_x = send([take(v, (1 - grp) ^ top) for v in sums], MASK_X)

    head = add_z(head, head_z)
    head_y = queued(take(head, 1 - y).astype(BF16), MASK_Y)

    sums = add([take(v, grp ^ top) for v in sums], hid_x)
    if n_z == 4:
        near = [jnp.stack([take(v, z ^ 1 ^ low_even), take(v, z ^ 2 ^ low_even)]) for v in sums]
        hid_z = send(near, 4)
        far = add([take(v, z ^ 3 ^ low_even) for v in sums], hid_z[1])
        out = add([take(v, z ^ low_even) for v in sums], hid_z[0])
        hid_z = send(far, 12)

    head = take(head, y) + wide(head_y)
    kept = take(head, core)
    came = queued(take(head, 1 - core), MASK_C)
    head = jnp.where(
        core == 0, jnp.concatenate([kept, came], 1), jnp.concatenate([came, kept], 1)
    )
    grad_head = head[:n_head].T
    feature = jnp.sum(head[n_head])

    if n_z == 4:
        out = add(out, hid_z)
    else:
        out = [take(v, z ^ low_even) for v in sums]
        for k in range(1, n_z):
            out = add(out, send([take(v, z ^ k ^ low_even) for v in sums], 4 * k))
    grad_up, grad_down = out[0].T, out[1]

    loss = (feature + contrast) / (positive.shape[0] * PATCHES)
    return (loss, grad_up, grad_down, grad_head, grad_proj)


def solution(mesh):
    placed = (
        P("dp", None),
        P(),
        P("dp", "grp"),
        P("dp", "grp"),
        P("dp", None),
        P(),
        P(None, BOTH),
        P(BOTH, None),
        P(None, BOTH),
        P(None, BOTH),
        P(BOTH, None),
        P(),
        P(),
    )
    return jax.shard_map(
        local,
        mesh=mesh,
        in_specs=placed,
        out_specs=(
            P(),
            P(None, BOTH),
            P(BOTH, None),
            P(None, BOTH),
            P(None, BOTH),
        ),
        check_vma=False,
    )
```
